32 devices in a mesh: seq: 16 (over z, y, core), head: 2 (over x).
Axes of the slice: x: 2, y: 2, z: 4, core: 2. Of those that a mesh axis runs over, the one named last changes fastest.
Arguments:
- query: bfloat16 [4096, 8, 4, 128], P('seq', None, 'head'), may hold values from -40 to 40
- key_in: bfloat16 [4096, 8, 128], P('seq', 'head'), may hold values from -16 to 16
- value: bfloat16 [4096, 8, 128], P('seq', 'head'), may hold values from -6 to 6
- grad_out: bfloat16 [4096, 8, 4, 128], P('seq', None, 'head'), may hold values from -6 to 6
- band_width: int32 [8, 4], P(None, 'head'), may hold values from 1 to 2, as said below
- stride_bits: int32 [4], replicated, may hold values from 0 to 3, each once
- partner_table: int32 [32, 4], P('seq'), may hold values from 0 to 1
Outputs:
- attn_out: bfloat16 [4096, 8, 4, 128], P('seq', None, 'head')
- grad_query: bfloat16 [4096, 8, 4, 128], P('seq', None, 'head')
- grad_key: bfloat16 [4096, 8, 128], P('seq', 'head')
- grad_value: bfloat16 [4096, 8, 128], P('seq', 'head')
The draws below stay inside these ranges and needn't reach their ends.
Inputs may be any that keep to these rules, and one draw needn't show every extreme that they name: `band_width`: some query head has band width 1 and some has 2. `stride_bits`: each section flips a different bit.
All inputs are finite; a program needn't handle non-finite values.
Results may differ from the reference program's by a relative error of at most 0.023.
Values may be sent and summed in bfloat16 or wider, within the bound.
A program may use at most 192 MiB of HBM per device.

```python
import jax
import jax.numpy as jnp
from jax import lax

HD = 128
KVH = 8
GROUP = 4
BLOCK = 128
BANDMAX = 2
TOK_DEV = 256
TOKENS = 4096
LEVELS = 4
NB = 32


def pair_draw(key):
    query_seed = jax.random.fold_in(key, 101)
    key_seed = jax.random.fold_in(key, 102)
    query_rows = jax.random.normal(query_seed, (TOKENS, KVH, GROUP, HD), jnp.float32)
    key_rows = jax.random.normal(key_seed, (TOKENS, KVH, HD), jnp.float32)
    return (jnp.clip(query_rows, -40.0, 40.0), jnp.clip(key_rows, -16.0, 16.0))


def draw_query(key, part):
    return pair_draw(key)[0].astype(jnp.bfloat16)


def draw_key_in(key, part):
    return pair_draw(key)[1].astype(jnp.bfloat16)


def draw_band_width(key, part):
    count = KVH * GROUP
    order = jax.random.permutation(jax.random.fold_in(key, 201), count)
    rough = jax.random.randint(jax.random.fold_in(key, 202), (count,), 1, BANDMAX + 1)
    widths = jnp.where(order == 0, 1, jnp.where(order == 1, BANDMAX, rough))
    return widths.reshape(KVH, GROUP).astype(jnp.int32)


def touch_ends(result, own_key, low, high):
    extent = result.shape
    index_at = [jax.random.randint(jax.random.fold_in(own_key, axis), (), 0, extent[axis]) for axis in range(len(extent))]
    result = result.at[tuple(index_at)].set(low)
    longest = extent.index(max(extent))
    index_at[longest] = (index_at[longest] + 1) % extent[longest]
    return result.at[tuple(index_at)].set(high)


def shard_levels(stream_key, dims, pieces, low, top_value):
    def one(position, blocks):
        draws = jax.random.uniform(jax.random.fold_in(jax.random.fold_in(stream_key, 6), position), (blocks,), jnp.float32, low / len(pieces), top_value / len(pieces))
        return jnp.repeat(jnp.exp(draws), dims[position] // blocks).reshape((-1,) + (1,) * (len(dims) - position - 1))

    gain = one(*pieces[0])
    for cut in pieces[1:]:
        gain = gain * one(*cut)
    return gain


def centred(own_key, extent, deviation, bound, cuts=(), kind=jnp.bfloat16):
    array = deviation * jax.random.normal(own_key, extent, jnp.float32)
    if cuts:
        array = array * shard_levels(own_key, extent, cuts, -0.22, 0.18)
    return jnp.clip(array, -bound, bound).astype(kind)


def setup_inputs(seed: int = 0) -> dict:
    seeds = jax.random.split(jax.random.key(seed), 8)
    query = draw_query(jax.random.fold_in(seeds[7], 71), 0)
    key_in = draw_key_in(jax.random.fold_in(seeds[7], 71), 0)
    value = centred(seeds[2], (TOKENS, KVH, HD), 1.0, 6.0, ((0, 16), (1, 2)))
    grad_out = centred(seeds[3], (TOKENS, KVH, GROUP, HD), 1.0, 6.0, ((0, 16), (2, 2)))
    band_width = draw_band_width(jax.random.fold_in(seeds[7], 71), 0)
    stride_bits = jax.random.permutation(seeds[5], LEVELS).astype(jnp.int32)
    partner_table = touch_ends(jax.random.randint(seeds[6], (NB, LEVELS), 0, TOK_DEV // BLOCK), jax.random.fold_in(seeds[6], 1), 0, (TOK_DEV // BLOCK) - 1).astype(jnp.int32)
    return dict(query=query, key_in=key_in, value=value, grad_out=grad_out, band_width=band_width, stride_bits=stride_bits, partner_table=partner_table)


def reference(query, key_in, value, grad_out, band_width, stride_bits, partner_table):
    tokens = query.shape[0]
    kv_heads = key_in.shape[1]
    groups = query.shape[2]
    head_dim = query.shape[3]
    all_blocks = tokens // BLOCK
    local_blocks = TOK_DEV // BLOCK
    half_band = BANDMAX - 1
    levels = stride_bits.shape[0]
    score_scale = head_dim ** -0.5
    blocks = jnp.arange(all_blocks, dtype=jnp.int32)
    offsets = jnp.arange(-half_band, half_band + 1, dtype=jnp.int32)
    band_index = blocks[:, None] + offsets[None, :]
    edge_valid = (band_index >= 0) & (band_index < all_blocks)
    owner_device = blocks // local_blocks
    flips = jnp.left_shift(jnp.int32(1), stride_bits.astype(jnp.int32))
    partner_device = jnp.bitwise_xor(owner_device[:, None], flips[None, :])
    partner_index = (partner_device * local_blocks + partner_table).astype(jnp.int32)
    key_index = jnp.concatenate([jnp.clip(band_index, 0, all_blocks - 1), partner_index], axis=1).astype(jnp.int32)
    width_valid = jnp.abs(offsets)[None, None, :] < band_width[:, :, None]
    key_blocks = key_in.reshape(all_blocks, BLOCK, kv_heads, head_dim)
    value_blocks = value.reshape(all_blocks, BLOCK, kv_heads, head_dim)

    def block_step(totals, block_num):
        grad_keys, grad_values = totals
        block_list = key_index[block_num]
        key_rows = key_blocks[block_list].reshape(-1, kv_heads, head_dim).astype(jnp.float32)
        value_rows = value_blocks[block_list].reshape(-1, kv_heads, head_dim).astype(jnp.float32)
        start = (block_num * BLOCK).astype(jnp.int32)
        query_rows = lax.dynamic_slice_in_dim(query, start, BLOCK, 0).astype(jnp.float32)
        grad_rows = lax.dynamic_slice_in_dim(grad_out, start, BLOCK, 0).astype(jnp.float32)
        band_valid = width_valid & edge_valid[block_num][None, None, :]
        valid_keys = jnp.concatenate([band_valid, jnp.ones((kv_heads, groups, levels), jnp.bool_)], axis=-1)
        valid_keys = jnp.repeat(valid_keys, BLOCK, axis=-1)
        scores = jnp.einsum('qhgd,khd->hgqk', query_rows, key_rows) * score_scale
        scores = jnp.where(valid_keys[:, :, None, :], scores, -jnp.inf)
        row_max = jnp.max(scores, axis=-1, keepdims=True)
        log_total = row_max + jnp.log(jnp.sum(jnp.exp(scores - row_max), axis=-1, keepdims=True))
        probability = jnp.exp(scores - log_total)
        weights = probability.astype(jnp.bfloat16).astype(jnp.float32)
        output = jnp.einsum('hgqk,khd->qhgd', weights, value_rows).astype(jnp.bfloat16)
        row_delta = jnp.sum(grad_rows * output.astype(jnp.float32), axis=-1)
        grad_prob = jnp.einsum('qhgd,khd->hgqk', grad_rows, value_rows)
        grad_score = (probability * (grad_prob - jnp.transpose(row_delta, (1, 2, 0))[..., None])).astype(jnp.bfloat16).astype(jnp.float32)
        grad_q = (jnp.einsum('hgqk,khd->qhgd', grad_score, key_rows) * score_scale).astype(jnp.bfloat16)
        grad_k = jnp.einsum('hgqk,qhgd->khd', grad_score, query_rows) * score_scale
        grad_v = jnp.einsum('hgqk,qhgd->khd', weights, grad_rows)
        grad_keys = grad_keys.at[block_list].add(grad_k.reshape(-1, BLOCK, kv_heads, head_dim))
        grad_values = grad_values.at[block_list].add(grad_v.reshape(-1, BLOCK, kv_heads, head_dim))
        return (grad_keys, grad_values), (output, grad_q)

    zero_grads = jnp.zeros((all_blocks, BLOCK, kv_heads, head_dim), jnp.float32)
    (grad_keys, grad_values), (outputs, grad_queries) = lax.scan(block_step, (zero_grads, zero_grads), blocks)
    return (outputs.reshape(query.shape), grad_queries.reshape(query.shape),
            grad_keys.reshape(key_in.shape).astype(jnp.bfloat16), grad_values.reshape(value.shape).astype(jnp.bfloat16))
```

```python
import functools
import math

import jax
import jax.numpy as jnp
from jax import lax
from jax.experimental import pallas as pl
from jax.experimental.pallas import tpu as pltpu
from jax.sharding import PartitionSpec as P

BLOCK = 128
MESH = pl.DeviceIdType.MESH
NEG = -1e30


def dot(a, b, ca, cb):
    return lax.dot_general(a, b, (((ca,), (cb,)), ((), ())), preferred_element_type=jnp.float32)


def kernel(
    n_seq,
    levels,
    heads,
    table_ref,
    bits_ref,
    query_ref,
    grad_ref,
    kv_ref,
    width_ref,
    out_ref,
    gq_ref,
    dkv_ref,
    query_in,
    grad_in,
    width_in,
    kv_lev,
    kv_rim,
    kv_cat,
    terms,
    out_send,
    gq_send,
    lev_send,
    lev_recv,
    rim_send,
    rim_recv,
    own_sum,
    width_sem,
    qg_sem,
    kv_sem,
    rim_sem,
    og_sem,
    dlev_sem,
    drim_sem,
):
    dev = lax.axis_index("seq")
    head = lax.axis_index("head")
    other = 1 - head
    mine0 = head * heads
    other0 = other * heads
    span = 3
    slots = span + levels
    scale = 128.0 ** (-0.5)
    exp_scale = scale * math.log2(math.e)
    has_low = dev > 0
    has_high = dev < n_seq - 1

    def flip(level):
        step = 1 << level
        return dev + step - 2 * step * (lax.div(dev, step) % 2)

    def remote(src, dst, sems, index, target):
        return pltpu.make_async_remote_copy(
            src_ref=src,
            dst_ref=dst,
            send_sem=sems.at[(0,) + index],
            recv_sem=sems.at[(1,) + index],
            device_id=target,
            device_id_type=MESH,
        )

    barrier = pltpu.get_barrier_semaphore()
    pl.semaphore_signal(barrier, inc=1, device_id=(dev, other), device_id_type=MESH)
    for level in range(levels):
        pl.semaphore_signal(barrier, inc=1, device_id=(flip(level), head), device_id_type=MESH)

    @pl.when(has_low)
    def _():
        pl.semaphore_signal(barrier, inc=1, device_id=(dev - 1, head), device_id_type=MESH)

    @pl.when(has_high)
    def _():
        pl.semaphore_signal(barrier, inc=1, device_id=(dev + 1, head), device_id_type=MESH)

    edges = jnp.where(has_low, 1, 0) + jnp.where(has_high, 1, 0)
    pl.semaphore_wait(barrier, levels + 1 + edges)

    def width_copy():
        return remote(width_ref.at[pl.ds(other0, heads)], width_in, width_sem, (), (dev, other))

    def qg_copies(j):
        return [
            remote(query_ref.at[other0 + j], query_in.at[j], qg_sem, (0, j), (dev, other)),
            remote(grad_ref.at[other0 + j], grad_in.at[j], qg_sem, (1, j), (dev, other)),
        ]

    def kv_copy(j, level):
        return remote(
            kv_ref.at[j], kv_lev.at[level, j], kv_sem, (level, j), (flip(level), head)
        )

    def rim_up(j):
        return remote(
            kv_ref.at[j, :, pl.ds(BLOCK, BLOCK)], kv_rim.at[0, j], rim_sem, (0, j), (dev + 1, head)
        )

    def rim_down(j):
        return remote(
            kv_ref.at[j, :, pl.ds(0, BLOCK)], kv_rim.at[1, j], rim_sem, (1, j), (dev - 1, head)
        )

    def og_copies(j):
        return [
            remote(out_send.at[j], out_ref.at[mine0 + j], og_sem, (0, j), (dev, other)),
            remote(gq_send.at[j], gq_ref.at[mine0 + j], og_sem, (1, j), (dev, other)),
        ]

    def dlev_copy(j, level):
        return remote(
            lev_send.at[level, j], lev_recv.at[level, j], dlev_sem, (level, j), (flip(level), head)
        )

    def drim_up(j):
        return remote(rim_send.at[0, j], rim_recv.at[0, j], drim_sem, (0, j), (dev + 1, head))

    def drim_down(j):
        return remote(rim_send.at[1, j], rim_recv.at[1, j], drim_sem, (1, j), (dev - 1, head))

    width_copy().start()

    def send_head(j, carry):
        for level in reversed(range(levels)):
            kv_copy(j, level).start()

        @pl.when(has_high)
        def _():
            rim_up(j).start()

        @pl.when(has_low)
        def _():
            rim_down(j).start()

        for copy in qg_copies(j):
            copy.start()
        return carry

    lax.fori_loop(0, heads, send_head, 0)

    @pl.when(jnp.logical_not(has_low))
    def _():
        kv_rim[0] = jnp.zeros_like(kv_rim[0])
        rim_recv[0] = jnp.zeros_like(rim_recv[0])

    @pl.when(jnp.logical_not(has_high))
    def _():
        kv_rim[1] = jnp.zeros_like(kv_rim[1])
        rim_recv[1] = jnp.zeros_like(rim_recv[1])

    width_copy().wait_recv()

    chosen = [
        [
            sum(
                (
                    jnp.where(bits_ref[s] == level, table_ref[block, s], 0)
                    for s in range(levels)
                ),
                jnp.int32(0),
            )
            for level in range(levels)
        ]
        for block in range(2)
    ]

    def one_head(j, carry):
        for copy in qg_copies(j):
            copy.wait_recv()
        for level in range(levels):
            kv_copy(j, level).wait_recv()

        @pl.when(has_low)
        def _():
            rim_up(j).wait_recv()

        @pl.when(has_high)
        def _():
            rim_down(j).wait_recv()

        for block in range(2):
            low_ok = has_low if block == 0 else True
            high_ok = has_high if block == 1 else True
            rows = pl.ds(block * 2 * BLOCK, 2 * BLOCK)
            for part in range(2):
                own = kv_ref[j, part]
                band = (
                    [kv_rim[0, j, part], own[:BLOCK], own[BLOCK:]]
                    if block == 0
                    else [own[:BLOCK], own[BLOCK:], kv_rim[1, j, part]]
                )
                for slot in range(span):
                    kv_cat[part, slot * BLOCK : (slot + 1) * BLOCK] = band[slot]
                for level in range(levels):
                    got = kv_lev[level, j, part]
                    pick = jnp.where(chosen[block][level] == 0, got[:BLOCK], got[BLOCK:])
                    kv_cat[part, (span + level) * BLOCK : (span + level + 1) * BLOCK] = pick
            keys = kv_cat[0]
            values = kv_cat[1]
            dk = None
            dv = None
            for source in range(2):
                if source == 0:
                    q = query_ref[mine0 + j, rows]
                    g = grad_ref[mine0 + j, rows]
                    width = width_ref[mine0 + j]
                else:
                    q = query_in[j, rows]
                    g = grad_in[j, rows]
                    width = width_in[j]
                wide = width > 1.5
                low_bias = jnp.where(wide, 0.0, NEG)
                high_bias = low_bias
                if block == 0:
                    low_bias = low_bias + jnp.where(low_ok, 0.0, NEG)
                else:
                    high_bias = high_bias + jnp.where(high_ok, 0.0, NEG)
                reps = 2 * BLOCK // 8
                low_bias = jnp.concatenate([low_bias] * reps, axis=0)
                high_bias = jnp.concatenate([high_bias] * reps, axis=0)
                scores = dot(q, keys, 1, 1)
                scores = jnp.concatenate(
                    [
                        scores[:, :BLOCK] + low_bias,
                        scores[:, BLOCK : 2 * BLOCK],
                        scores[:, 2 * BLOCK : 3 * BLOCK] + high_bias,
                        scores[:, 3 * BLOCK :],
                    ],
                    axis=1,
                )
                top = jnp.max(scores, axis=1, keepdims=True)
                prob = jnp.exp2((scores - top) * exp_scale)
                prob = prob * (1.0 / jnp.sum(prob, axis=1, keepdims=True))
                weights = prob.astype(jnp.bfloat16)
                out = dot(weights, values, 1, 0).astype(jnp.bfloat16)
                delta = jnp.sum(
                    g.astype(jnp.float32) * out.astype(jnp.float32), axis=1, keepdims=True
                )
                ds = (prob * (dot(g, values, 1, 1) - delta)).astype(jnp.bfloat16)
                gq = (dot(ds, keys, 1, 0) * scale).astype(jnp.bfloat16)
                if source == 0:
                    out_ref[mine0 + j, rows] = out
                    gq_ref[mine0 + j, rows] = gq
                else:
                    out_send[j, rows] = out
                    gq_send[j, rows] = gq
                dk_part = dot(ds, q, 0, 0)
                dv_part = dot(weights, g, 0, 0)
                dk = dk_part if dk is None else dk + dk_part
                dv = dv_part if dv is None else dv + dv_part
            terms[block, 0] = dk * scale
            terms[block, 1] = dv

        for copy in og_copies(j):
            copy.start()
        for level in reversed(range(levels)):
            cols = pl.ds((span + level) * BLOCK, BLOCK)
            for part in range(2):
                a = terms[0, part, cols]
                b = terms[1, part, cols]
                for target in range(2):
                    piece = jnp.where(chosen[0][level] == target, a, 0.0) + jnp.where(
                        chosen[1][level] == target, b, 0.0
                    )
                    lev_send[level, j, part, target * BLOCK : (target + 1) * BLOCK] = piece.astype(
                        jnp.bfloat16
                    )
            dlev_copy(j, level).start()
        for part in range(2):
            rim_send[1, j, part] = terms[0, part, :BLOCK].astype(jnp.bfloat16)
            rim_send[0, j, part] = terms[1, part, 2 * BLOCK : 3 * BLOCK].astype(jnp.bfloat16)
            own_sum[j, part, :BLOCK] = terms[0, part, BLOCK : 2 * BLOCK] + terms[1, part, :BLOCK]
            own_sum[j, part, BLOCK:] = (
                terms[0, part, 2 * BLOCK : 3 * BLOCK] + terms[1, part, BLOCK : 2 * BLOCK]
            )

        @pl.when(has_high)
        def _():
            drim_up(j).start()

        @pl.when(has_low)
        def _():
            drim_down(j).start()

        return carry

    lax.fori_loop(0, heads, one_head, 0)

    def finish(j, carry):
        for level in range(levels):
            dlev_copy(j, level).wait_recv()

        @pl.when(has_low)
        def _():
            drim_up(j).wait_recv()

        @pl.when(has_high)
        def _():
            drim_down(j).wait_recv()

        for part in range(2):
            total = own_sum[j, part]
            for level in range(levels):
                total = total + lev_recv[level, j, part].astype(jnp.float32)
            first = total[:BLOCK] + rim_recv[0, j, part].astype(jnp.float32)
            last = total[BLOCK:] + rim_recv[1, j, part].astype(jnp.float32)
            dkv_ref[part, j, :BLOCK] = first.astype(jnp.bfloat16)
            dkv_ref[part, j, BLOCK:] = last.astype(jnp.bfloat16)
        for copy in og_copies(j):
            copy.wait_recv()
        return carry

    lax.fori_loop(0, heads, finish, 0)

    def drain(j, carry):
        for copy in qg_copies(j) + og_copies(j):
            copy.wait_send()
        for level in range(levels):
            kv_copy(j, level).wait_send()
            dlev_copy(j, level).wait_send()

        @pl.when(has_high)
        def _():
            rim_up(j).wait_send()
            drim_up(j).wait_send()

        @pl.when(has_low)
        def _():
            rim_down(j).wait_send()
            drim_down(j).wait_send()

        return carry

    lax.fori_loop(0, heads, drain, 0)
    width_copy().wait_send()


def shards(query, key_in, value, grad_out, band_width, stride_bits, partner_table):
    tokens, kv_heads, groups, dim = query.shape
    heads = key_in.shape[1]
    n_seq = lax.axis_size("seq")
    levels = n_seq.bit_length() - 1
    rows = tokens * groups
    bf16 = jnp.bfloat16
    f32 = jnp.float32
    q = jnp.transpose(query, (1, 0, 2, 3)).reshape(kv_heads, rows, dim)
    g = jnp.transpose(grad_out, (1, 0, 2, 3)).reshape(kv_heads, rows, dim)
    kv = jnp.transpose(jnp.stack([key_in, value]), (2, 0, 1, 3))
    width = jnp.tile(band_width.astype(f32), (1, 8 // groups))
    width = jnp.broadcast_to(width[:, :, None], (kv_heads, 8, 128))
    vmem = pl.BlockSpec(memory_space=pltpu.VMEM)
    smem = pl.BlockSpec(memory_space=pltpu.SMEM)
    slots = 3 + levels
    dma = pltpu.SemaphoreType.DMA
    out, gq, dkv = pl.pallas_call(
        functools.partial(kernel, n_seq, levels, heads),
        out_shape=(
            jax.ShapeDtypeStruct((kv_heads, rows, dim), bf16),
            jax.ShapeDtypeStruct((kv_heads, rows, dim), bf16),
            jax.ShapeDtypeStruct((2, heads, tokens, dim), bf16),
        ),
        in_specs=[smem, smem, vmem, vmem, vmem, vmem],
        out_specs=(vmem, vmem, vmem),
        scratch_shapes=[
            pltpu.VMEM((heads, rows, dim), bf16),
            pltpu.VMEM((heads, rows, dim), bf16),
            pltpu.VMEM((heads, 8, 128), f32),
            pltpu.VMEM((levels, heads, 2, tokens, dim), bf16),
            pltpu.VMEM((2, heads, 2, BLOCK, dim), bf16),
            pltpu.VMEM((2, slots * BLOCK, dim), bf16),
            pltpu.VMEM((2, 2, slots * BLOCK, dim), f32),
            pltpu.VMEM((heads, rows, dim), bf16),
            pltpu.VMEM((heads, rows, dim), bf16),
            pltpu.VMEM((levels, heads, 2, tokens, dim), bf16),
            pltpu.VMEM((levels, heads, 2, tokens, dim), bf16),
            pltpu.VMEM((2, heads, 2, BLOCK, dim), bf16),
            pltpu.VMEM((2, heads, 2, BLOCK, dim), bf16),
            pltpu.VMEM((heads, 2, tokens, dim), f32),
            dma((2,)),
            dma((2, 2, heads)),
            dma((2, levels, heads)),
            dma((2, 2, heads)),
            dma((2, 2, heads)),
            dma((2, levels, heads)),
            dma((2, 2, heads)),
        ],
        compiler_params=pltpu.CompilerParams(
            collective_id=0, has_side_effects=True, vmem_limit_bytes=56 * 1024 * 1024
        ),
    )(partner_table, stride_bits, q, g, kv, width)
    out = jnp.transpose(out.reshape(kv_heads, tokens, groups, dim), (1, 0, 2, 3))
    gq = jnp.transpose(gq.reshape(kv_heads, tokens, groups, dim), (1, 0, 2, 3))
    dkv = jnp.transpose(dkv, (0, 2, 1, 3))
    return out, gq, dkv[0], dkv[1]


def solution(mesh):
    placed = (
        P("seq", None, "head", None),
        P("seq", "head", None),
        P("seq", "head", None),
        P("seq", None, "head", None),
        P(None, "head"),
        P(),
        P("seq", None),
    )
    return jax.shard_map(
        shards,
        mesh=mesh,
        in_specs=placed,
        out_specs=(
            P("seq", None, "head", None),
            P("seq", None, "head", None),
            P("seq", "head", None),
            P("seq", "head", None),
        ),
        check_vma=False,
    )
```

```python
import functools
import math

import jax
import jax.numpy as jnp
from jax import lax
from jax.experimental import pallas as pl
from jax.experimental.pallas import tpu as pltpu
from jax.sharding import PartitionSpec as P

BLOCK = 128
MESH = pl.DeviceIdType.MESH
NEG = -1e30


def dot(a, b, ca, cb):
    return lax.dot_general(a, b, (((ca,), (cb,)), ((), ())), preferred_element_type=jnp.float32)


def kernel(
    n_seq,
    levels,
    heads,
    groups,
    table_ref,
    bits_ref,
    query_ref,
    grad_ref,
    key_ref,
    value_ref,
    width_ref,
    out_ref,
    gq_ref,
    dk_ref,
    dv_ref,
    kv_ref,
    query_in,
    grad_in,
    width_in,
    kv_lev,
    kv_rim,
    kv_cat,
    terms,
    out_send,
    gq_send,
    lev_send,
    lev_recv,
    rim_send,
    rim_recv,
    own_sum,
    width_sem,
    qg_sem,
    kv_sem,
    rim_sem,
    og_sem,
    dlev_sem,
    drim_sem,
):
    dev = lax.axis_index("seq")
    head = lax.axis_index("head")
    other = 1 - head
    mine0 = head * heads
    other0 = other * heads
    span = 3
    slots = span + levels
    scale = 128.0 ** (-0.5)
    exp_scale = scale * math.log2(math.e)
    has_low = dev > 0
    has_high = dev < n_seq - 1

    def flip(level):
        step = 1 << level
        return dev + step - 2 * step * (lax.div(dev, step) % 2)

    def remote(src, dst, sems, index, target):
        return pltpu.make_async_remote_copy(
            src_ref=src,
            dst_ref=dst,
            send_sem=sems.at[(0,) + index],
            recv_sem=sems.at[(1,) + index],
            device_id=target,
            device_id_type=MESH,
        )

    barrier = pltpu.get_barrier_semaphore()
    pl.semaphore_signal(barrier, inc=1, device_id=(dev, other), device_id_type=MESH)
    for level in range(levels):
        pl.semaphore_signal(barrier, inc=1, device_id=(flip(level), head), device_id_type=MESH)

    @pl.when(has_low)
    def _():
        pl.semaphore_signal(barrier, inc=1, device_id=(dev - 1, head), device_id_type=MESH)

    @pl.when(has_high)
    def _():
        pl.semaphore_signal(barrier, inc=1, device_id=(dev + 1, head), device_id_type=MESH)

    edges = jnp.where(has_low, 1, 0) + jnp.where(has_high, 1, 0)
    pl.semaphore_wait(barrier, levels + 1 + edges)

    def width_copy():
        return remote(width_ref, width_in, width_sem, (), (dev, other))

    def qg_copies(j):
        return [
            remote(query_ref.at[other0 + j], query_in.at[j], qg_sem, (0, j), (dev, other)),
            remote(grad_ref.at[other0 + j], grad_in.at[j], qg_sem, (1, j), (dev, other)),
        ]

    def kv_copy(j, level):
        return remote(
            kv_ref.at[j], kv_lev.at[level, j], kv_sem, (level, j), (flip(level), head)
        )

    def rim_up(j):
        return remote(
            kv_ref.at[j, :, pl.ds(BLOCK, BLOCK)], kv_rim.at[0, j], rim_sem, (0, j), (dev + 1, head)
        )

    def rim_down(j):
        return remote(
            kv_ref.at[j, :, pl.ds(0, BLOCK)], kv_rim.at[1, j], rim_sem, (1, j), (dev - 1, head)
        )

    def og_copies(j, block):
        rows = pl.ds(block * 2 * BLOCK, 2 * BLOCK)
        return [
            remote(
                out_send.at[j, rows], out_ref.at[mine0 + j, rows], og_sem, (0, block, j), (dev, other)
            ),
            remote(
                gq_send.at[j, rows], gq_ref.at[mine0 + j, rows], og_sem, (1, block, j), (dev, other)
            ),
        ]

    def dlev_copy(j, level):
        return remote(
            lev_send.at[level, j], lev_recv.at[level, j], dlev_sem, (level, j), (flip(level), head)
        )

    def drim_up(j):
        return remote(rim_send.at[0, j], rim_recv.at[0, j], drim_sem, (0, j), (dev + 1, head))

    def drim_down(j):
        return remote(rim_send.at[1, j], rim_recv.at[1, j], drim_sem, (1, j), (dev - 1, head))

    def send_head(j):
        kv_ref[j, 0] = key_ref[j]
        kv_ref[j, 1] = value_ref[j]

        @pl.when(has_high)
        def _():
            rim_up(j).start()

        @pl.when(has_low)
        def _():
            rim_down(j).start()

        for level in reversed(range(levels)):
            kv_copy(j, level).start()
        for copy in qg_copies(j):
            copy.start()

    send_head(0)
    width_copy().start()

    @pl.when(jnp.logical_not(has_low))
    def _():
        kv_rim[0] = jnp.zeros_like(kv_rim[0])
        rim_recv[0] = jnp.zeros_like(rim_recv[0])

    @pl.when(jnp.logical_not(has_high))
    def _():
        kv_rim[1] = jnp.zeros_like(kv_rim[1])
        rim_recv[1] = jnp.zeros_like(rim_recv[1])

    width_copy().wait_recv()

    chosen = [
        [
            sum(
                (
                    jnp.where(bits_ref[s] == level, table_ref[block, s], 0)
                    for s in range(levels)
                ),
                jnp.int32(0),
            )
            for level in range(levels)
        ]
        for block in range(2)
    ]

    def one_head(j, carry):
        for level in range(min(2, levels)):
            kv_copy(j, level).wait_recv()

        @pl.when(j == 0)
        def _():
            send_head(1)

        for level in range(min(2, levels), levels):
            kv_copy(j, level).wait_recv()
        for copy in qg_copies(j):
            copy.wait_recv()

        @pl.when(has_low)
        def _():
            rim_up(j).wait_recv()

        @pl.when(has_high)
        def _():
            rim_down(j).wait_recv()

        @pl.when(j + 2 < heads)
        def _():
            send_head(j + 2)

        for block in range(2):
            low_ok = has_low if block == 0 else True
            high_ok = has_high if block == 1 else True
            rows = pl.ds(block * 2 * BLOCK, 2 * BLOCK)
            for part in range(2):
                own = kv_ref[j, part]
                band = (
                    [kv_rim[0, j, part], own[:BLOCK], own[BLOCK:]]
                    if block == 0
                    else [own[:BLOCK], own[BLOCK:], kv_rim[1, j, part]]
                )
                for slot in range(span):
                    kv_cat[part, slot * BLOCK : (slot + 1) * BLOCK] = band[slot]
                for level in range(levels):
                    got = kv_lev[level, j, part]
                    pick = jnp.where(chosen[block][level] == 0, got[:BLOCK], got[BLOCK:])
                    kv_cat[part, (span + level) * BLOCK : (span + level + 1) * BLOCK] = pick
            keys = kv_cat[0]
            values = kv_cat[1]
            dk = None
            dv = None
            for source in range(2):
                if source == 0:
                    q = query_ref[mine0 + j, rows]
                    g = grad_ref[mine0 + j, rows]
                    width = width_ref[pl.ds(mine0 + j, 1)]
                else:
                    q = query_in[j, rows]
                    g = grad_in[j, rows]
                    width = width_in[pl.ds(mine0 + j, 1)]
                lane = lax.broadcasted_iota(jnp.int32, (8, 128), 0) % groups
                wide = jnp.zeros((8, 128), jnp.int32)
                for group in range(groups):
                    wide = jnp.where(lane == group, width[:, group : group + 1], wide)
                wide = wide > 1
                low_bias = jnp.where(wide, 0.0, NEG)
                high_bias = low_bias
                if block == 0:
                    low_bias = low_bias + jnp.where(low_ok, 0.0, NEG)
                else:
                    high_bias = high_bias + jnp.where(high_ok, 0.0, NEG)
                reps = 2 * BLOCK // 8
                low_bias = jnp.concatenate([low_bias] * reps, axis=0)
                high_bias = jnp.concatenate([high_bias] * reps, axis=0)
                scores = dot(q, keys, 1, 1)
                scores = jnp.concatenate(
                    [
                        scores[:, :BLOCK] + low_bias,
                        scores[:, BLOCK : 2 * BLOCK],
                        scores[:, 2 * BLOCK : 3 * BLOCK] + high_bias,
                        scores[:, 3 * BLOCK :],
                    ],
                    axis=1,
                )
                top = jnp.max(scores, axis=1, keepdims=True)
                prob = jnp.exp2((scores - top) * exp_scale)
                prob = prob * (1.0 / jnp.sum(prob, axis=1, keepdims=True))
                weights = prob.astype(jnp.bfloat16)
                out = dot(weights, values, 1, 0).astype(jnp.bfloat16)
                delta = jnp.sum(
                    g.astype(jnp.float32) * out.astype(jnp.float32), axis=1, keepdims=True
                )
                ds = (prob * (dot(g, values, 1, 1) - delta)).astype(jnp.bfloat16)
                gq = (dot(ds, keys, 1, 0) * scale).astype(jnp.bfloat16)
                if source == 0:
                    out_ref[mine0 + j, rows] = out
                    gq_ref[mine0 + j, rows] = gq
                else:
                    out_send[j, rows] = out
                    gq_send[j, rows] = gq
                dk_part = dot(ds, q, 0, 0)
                dv_part = dot(weights, g, 0, 0)
                dk = dk_part if dk is None else dk + dk_part
                dv = dv_part if dv is None else dv + dv_part
            terms[block, 0] = dk * scale
            terms[block, 1] = dv
            for copy in og_copies(j, block):
                copy.start()
            if block == 0:
                for part in range(2):
                    rim_send[1, j, part] = terms[0, part, :BLOCK].astype(jnp.bfloat16)

                @pl.when(has_low)
                def _():
                    drim_down(j).start()

            else:
                for part in range(2):
                    rim_send[0, j, part] = terms[1, part, 2 * BLOCK : 3 * BLOCK].astype(
                        jnp.bfloat16
                    )

                @pl.when(has_high)
                def _():
                    drim_up(j).start()

        for level in reversed(range(levels)):
            cols = pl.ds((span + level) * BLOCK, BLOCK)
            for part in range(2):
                a = terms[0, part, cols]
                b = terms[1, part, cols]
                for target in range(2):
                    piece = jnp.where(chosen[0][level] == target, a, 0.0) + jnp.where(
                        chosen[1][level] == target, b, 0.0
                    )
                    lev_send[level, j, part, target * BLOCK : (target + 1) * BLOCK] = piece.astype(
                        jnp.bfloat16
                    )
            dlev_copy(j, level).start()
        for part in range(2):
            own_sum[j, part, :BLOCK] = terms[0, part, BLOCK : 2 * BLOCK] + terms[1, part, :BLOCK]
            own_sum[j, part, BLOCK:] = (
                terms[0, part, 2 * BLOCK : 3 * BLOCK] + terms[1, part, BLOCK : 2 * BLOCK]
            )

        return carry

    lax.fori_loop(0, heads, one_head, 0)

    def finish(j, carry):
        for level in range(levels):
            dlev_copy(j, level).wait_recv()

        @pl.when(has_low)
        def _():
            drim_up(j).wait_recv()

        @pl.when(has_high)
        def _():
            drim_down(j).wait_recv()

        for part in range(2):
            total = own_sum[j, part]
            for level in range(levels):
                total = total + lev_recv[level, j, part].astype(jnp.float32)
            first = total[:BLOCK] + rim_recv[0, j, part].astype(jnp.float32)
            last = total[BLOCK:] + rim_recv[1, j, part].astype(jnp.float32)
            result = (dk_ref, dv_ref)[part]
            result[j, :BLOCK] = first.astype(jnp.bfloat16)
            result[j, BLOCK:] = last.astype(jnp.bfloat16)
        for block in range(2):
            for copy in og_copies(j, block):
                copy.wait_recv()
        return carry

    lax.fori_loop(0, heads, finish, 0)

    def drain(j, carry):
        for copy in qg_copies(j) + og_copies(j, 0) + og_copies(j, 1):
            copy.wait_send()
        for level in range(levels):
            kv_copy(j, level).wait_send()
            dlev_copy(j, level).wait_send()

        @pl.when(has_high)
        def _():
            rim_up(j).wait_send()
            drim_up(j).wait_send()

        @pl.when(has_low)
        def _():
            rim_down(j).wait_send()
            drim_down(j).wait_send()

        return carry

    lax.fori_loop(0, heads, drain, 0)
    width_copy().wait_send()


def shards(query, key_in, value, grad_out, band_width, stride_bits, partner_table):
    tokens, kv_heads, groups, dim = query.shape
    heads = key_in.shape[1]
    n_seq = lax.axis_size("seq")
    levels = n_seq.bit_length() - 1
    rows = tokens * groups
    bf16 = jnp.bfloat16
    f32 = jnp.float32
    q = jnp.transpose(query, (1, 0, 2, 3)).reshape(kv_heads, rows, dim)
    g = jnp.transpose(grad_out, (1, 0, 2, 3)).reshape(kv_heads, rows, dim)
    k = jnp.transpose(key_in, (1, 0, 2))
    v = jnp.transpose(value, (1, 0, 2))
    width = jnp.pad(band_width, ((0, 0), (0, 128 - groups)))
    vmem = pl.BlockSpec(memory_space=pltpu.VMEM)
    smem = pl.BlockSpec(memory_space=pltpu.SMEM)
    slots = 3 + levels
    dma = pltpu.SemaphoreType.DMA
    out, gq, dk, dv = pl.pallas_call(
        functools.partial(kernel, n_seq, levels, heads, groups),
        out_shape=(
            jax.ShapeDtypeStruct((kv_heads, rows, dim), bf16),
            jax.ShapeDtypeStruct((kv_heads, rows, dim), bf16),
            jax.ShapeDtypeStruct((heads, tokens, dim), bf16),
            jax.ShapeDtypeStruct((heads, tokens, dim), bf16),
        ),
        in_specs=[smem, smem] + [vmem] * 5,
        out_specs=(vmem,) * 4,
        scratch_shapes=[
            pltpu.VMEM((heads, 2, tokens, dim), bf16),
            pltpu.VMEM((heads, rows, dim), bf16),
            pltpu.VMEM((heads, rows, dim), bf16),
            pltpu.VMEM((kv_heads, 128), jnp.int32),
            pltpu.VMEM((levels, heads, 2, tokens, dim), bf16),
            pltpu.VMEM((2, heads, 2, BLOCK, dim), bf16),
            pltpu.VMEM((2, slots * BLOCK, dim), bf16),
            pltpu.VMEM((2, 2, slots * BLOCK, dim), f32),
            pltpu.VMEM((heads, rows, dim), bf16),
            pltpu.VMEM((heads, rows, dim), bf16),
            pltpu.VMEM((levels, heads, 2, tokens, dim), bf16),
            pltpu.VMEM((levels, heads, 2, tokens, dim), bf16),
            pltpu.VMEM((2, heads, 2, BLOCK, dim), bf16),
            pltpu.VMEM((2, heads, 2, BLOCK, dim), bf16),
            pltpu.VMEM((heads, 2, tokens, dim), f32),
            dma((2,)),
            dma((2, 2, heads)),
            dma((2, levels, heads)),
            dma((2, 2, heads)),
            dma((2, 2, 2, heads)),
            dma((2, levels, heads)),
            dma((2, 2, heads)),
        ],
        compiler_params=pltpu.CompilerParams(
            collective_id=0, has_side_effects=True, vmem_limit_bytes=34 * 1024 * 1024
        ),
    )(partner_table, stride_bits, q, g, k, v, width)
    out = jnp.transpose(out.reshape(kv_heads, tokens, groups, dim), (1, 0, 2, 3))
    gq = jnp.transpose(gq.reshape(kv_heads, tokens, groups, dim), (1, 0, 2, 3))
    return out, gq, jnp.transpose(dk, (1, 0, 2)), jnp.transpose(dv, (1, 0, 2))


def solution(mesh):
    placed = (
        P("seq", None, "head", None),
        P("seq", "head", None),
        P("seq", "head", None),
        P("seq", None, "head", None),
        P(None, "head"),
        P(),
        P("seq", None),
    )
    return jax.shard_map(
        shards,
        mesh=mesh,
        in_specs=placed,
        out_specs=(
            P("seq", None, "head", None),
            P("seq", None, "head", None),
            P("seq", "head", None),
            P("seq", "head", None),
        ),
        check_vma=False,
    )
```

```python
import functools
import math

import jax
import jax.numpy as jnp
from jax import lax
from jax.experimental import pallas as pl
from jax.experimental.pallas import tpu as pltpu
from jax.sharding import PartitionSpec as P

BLOCK = 128
MESH = pl.DeviceIdType.MESH
NEG = -1e30


def dot(a, b, ca, cb):
    return lax.dot_general(a, b, (((ca,), (cb,)), ((), ())), preferred_element_type=jnp.float32)


def kernel(
    n_seq,
    levels,
    heads,
    groups,
    table_ref,
    bits_ref,
    query_ref,
    grad_ref,
    key_ref,
    value_ref,
    width_ref,
    out_ref,
    gq_ref,
    dk_ref,
    dv_ref,
    kv_ref,
    query_in,
    grad_in,
    width_in,
    kv_lev,
    kv_rim,
    kv_cat,
    terms,
    out_send,
    gq_send,
    lev_send,
    lev_recv,
    rim_send,
    rim_recv,
    own_sum,
    width_sem,
    qg_sem,
    kv_sem,
    rim_sem,
    og_sem,
    dlev_sem,
    drim_sem,
):
    dev = lax.axis_index("seq")
    head = lax.axis_index("head")
    other = 1 - head
    mine0 = head * heads
    other0 = other * heads
    span = 3
    slots = span + levels
    scale = 128.0 ** (-0.5)
    exp_scale = scale * math.log2(math.e)
    has_low = dev > 0
    has_high = dev < n_seq - 1

    def flip(level):
        step = 1 << level
        return dev + step - 2 * step * (lax.div(dev, step) % 2)

    def remote(src, dst, sems, index, target):
        return pltpu.make_async_remote_copy(
            src_ref=src,
            dst_ref=dst,
            send_sem=sems.at[(0,) + index],
            recv_sem=sems.at[(1,) + index],
            device_id=target,
            device_id_type=MESH,
        )

    barrier = pltpu.get_barrier_semaphore()
    pl.semaphore_signal(barrier, inc=1, device_id=(dev, other), device_id_type=MESH)
    for level in range(levels):
        pl.semaphore_signal(barrier, inc=1, device_id=(flip(level), head), device_id_type=MESH)

    @pl.when(has_low)
    def _():
        pl.semaphore_signal(barrier, inc=1, device_id=(dev - 1, head), device_id_type=MESH)

    @pl.when(has_high)
    def _():
        pl.semaphore_signal(barrier, inc=1, device_id=(dev + 1, head), device_id_type=MESH)

    edges = jnp.where(has_low, 1, 0) + jnp.where(has_high, 1, 0)
    pl.semaphore_wait(barrier, levels + 1 + edges)

    def width_copy():
        return remote(width_ref, width_in, width_sem, (), (dev, other))

    def qg_copies(j):
        return [
            remote(query_ref.at[other0 + j], query_in.at[j], qg_sem, (0, j), (dev, other)),
            remote(grad_ref.at[other0 + j], grad_in.at[j], qg_sem, (1, j), (dev, other)),
        ]

    def kv_copy(j, level):
        return remote(
            kv_ref.at[j], kv_lev.at[level, j], kv_sem, (level, j), (flip(level), head)
        )

    def rim_up(j):
        return remote(
            kv_ref.at[j, :, pl.ds(BLOCK, BLOCK)], kv_rim.at[0, j], rim_sem, (0, j), (dev + 1, head)
        )

    def rim_down(j):
        return remote(
            kv_ref.at[j, :, pl.ds(0, BLOCK)], kv_rim.at[1, j], rim_sem, (1, j), (dev - 1, head)
        )

    def og_copies(j, block):
        rows = pl.ds(block * 2 * BLOCK, 2 * BLOCK)
        return [
            remote(
                out_send.at[j, rows], out_ref.at[mine0 + j, rows], og_sem, (0, block, j), (dev, other)
            ),
            remote(
                gq_send.at[j, rows], gq_ref.at[mine0 + j, rows], og_sem, (1, block, j), (dev, other)
            ),
        ]

    def dlev_copy(j, level):
        return remote(
            lev_send.at[level, j], lev_recv.at[level, j], dlev_sem, (level, j), (flip(level), head)
        )

    def drim_up(j):
        return remote(rim_send.at[0, j], rim_recv.at[0, j], drim_sem, (0, j), (dev + 1, head))

    def drim_down(j):
        return remote(rim_send.at[1, j], rim_recv.at[1, j], drim_sem, (1, j), (dev - 1, head))

    def send_head(j):
        kv_ref[j, 0] = key_ref[j]
        kv_ref[j, 1] = value_ref[j]

        @pl.when(has_high)
        def _():
            rim_up(j).start()

        @pl.when(has_low)
        def _():
            rim_down(j).start()

        for level in reversed(range(levels)):
            kv_copy(j, level).start()
        for copy in qg_copies(j):
            copy.start()

    send_head(0)
    width_copy().start()

    @pl.when(jnp.logical_not(has_low))
    def _():
        kv_rim[0] = jnp.zeros_like(kv_rim[0])
        rim_recv[0] = jnp.zeros_like(rim_recv[0])

    @pl.when(jnp.logical_not(has_high))
    def _():
        kv_rim[1] = jnp.zeros_like(kv_rim[1])
        rim_recv[1] = jnp.zeros_like(rim_recv[1])

    width_copy().wait_recv()

    chosen = [
        [
            sum(
                (
                    jnp.where(bits_ref[s] == level, table_ref[block, s], 0)
                    for s in range(levels)
                ),
                jnp.int32(0),
            )
            for level in range(levels)
        ]
        for block in range(2)
    ]

    def one_head(j, carry):
        for level in range(min(2, levels)):
            kv_copy(j, level).wait_recv()

        @pl.when(j == 0)
        def _():
            send_head(1)

        for level in range(min(2, levels), levels):
            kv_copy(j, level).wait_recv()
        for copy in qg_copies(j):
            copy.wait_recv()

        @pl.when(has_low)
        def _():
            rim_up(j).wait_recv()

        @pl.when(has_high)
        def _():
            rim_down(j).wait_recv()

        @pl.when(j + 2 < heads)
        def _():
            send_head(j + 2)

        for block in range(2):
            low_ok = has_low if block == 0 else True
            high_ok = has_high if block == 1 else True
            rows = pl.ds(block * 2 * BLOCK, 2 * BLOCK)
            for part in range(2):
                own = kv_ref[j, part]
                band = (
                    [kv_rim[0, j, part], own[:BLOCK], own[BLOCK:]]
                    if block == 0
                    else [own[:BLOCK], own[BLOCK:], kv_rim[1, j, part]]
                )
                for slot in range(span):
                    kv_cat[part, slot * BLOCK : (slot + 1) * BLOCK] = band[slot]
                for level in range(levels):
                    got = kv_lev[level, j, part]
                    pick = jnp.where(chosen[block][level] == 0, got[:BLOCK], got[BLOCK:])
                    kv_cat[part, (span + level) * BLOCK : (span + level + 1) * BLOCK] = pick
            keys = kv_cat[0]
            values = kv_cat[1]
            dk = None
            dv = None
            for source in range(2):
                if source == 0:
                    q = query_ref[mine0 + j, rows]
                    g = grad_ref[mine0 + j, rows]
                    width = width_ref[pl.ds(mine0 + j, 1)]
                else:
                    q = query_in[j, rows]
                    g = grad_in[j, rows]
                    width = width_in[pl.ds(mine0 + j, 1)]
                lane = lax.broadcasted_iota(jnp.int32, (8, 128), 0) % groups
                wide = jnp.zeros((8, 128), jnp.int32)
                for group in range(groups):
                    wide = jnp.where(lane == group, width[:, group : group + 1], wide)
                wide = wide > 1
                low_bias = jnp.where(wide, 0.0, NEG)
                high_bias = low_bias
                if block == 0:
                    low_bias = low_bias + jnp.where(low_ok, 0.0, NEG)
                else:
                    high_bias = high_bias + jnp.where(high_ok, 0.0, NEG)
                reps = 2 * BLOCK // 8
                low_bias = jnp.concatenate([low_bias] * reps, axis=0)
                high_bias = jnp.concatenate([high_bias] * reps, axis=0)
                scores = dot(q, keys, 1, 1)
                scores = jnp.concatenate(
                    [
                        scores[:, :BLOCK] + low_bias,
                        scores[:, BLOCK : 2 * BLOCK],
                        scores[:, 2 * BLOCK : 3 * BLOCK] + high_bias,
                        scores[:, 3 * BLOCK :],
                    ],
                    axis=1,
                )
                top = jnp.max(scores, axis=1, keepdims=True)
                prob = jnp.exp2((scores - top) * exp_scale)
                prob = prob * (1.0 / jnp.sum(prob, axis=1, keepdims=True))
                weights = prob.astype(jnp.bfloat16)
                out = dot(weights, values, 1, 0).astype(jnp.bfloat16)
                delta = jnp.sum(
                    g.astype(jnp.float32) * out.astype(jnp.float32), axis=1, keepdims=True
                )
                ds = (prob * (dot(g, values, 1, 1) - delta)).astype(jnp.bfloat16)
                gq = (dot(ds, keys, 1, 0) * scale).astype(jnp.bfloat16)
                if source == 0:
                    out_ref[mine0 + j, rows] = out
                    gq_ref[mine0 + j, rows] = gq
                else:
                    out_send[j, rows] = out
                    gq_send[j, rows] = gq
                dk_part = dot(q, ds, 0, 0)
                dv_part = dot(g, weights, 0, 0)
                dk = dk_part if dk is None else dk + dk_part
                dv = dv_part if dv is None else dv + dv_part
            terms[block, 0] = (dk * scale).T
            terms[block, 1] = dv.T
            for copy in og_copies(j, block):
                copy.start()
            if block == 0:
                for part in range(2):
                    rim_send[1, j, part] = terms[0, part, :BLOCK].astype(jnp.bfloat16)

                @pl.when(has_low)
                def _():
                    drim_down(j).start()

            else:
                for part in range(2):
                    rim_send[0, j, part] = terms[1, part, 2 * BLOCK : 3 * BLOCK].astype(
                        jnp.bfloat16
                    )

                @pl.when(has_high)
                def _():
                    drim_up(j).start()

        for level in reversed(range(levels)):
            cols = pl.ds((span + level) * BLOCK, BLOCK)
            for part in range(2):
                a = terms[0, part, cols]
                b = terms[1, part, cols]
                for target in range(2):
                    piece = jnp.where(chosen[0][level] == target, a, 0.0) + jnp.where(
                        chosen[1][level] == target, b, 0.0
                    )
                    lev_send[level, j, part, target * BLOCK : (target + 1) * BLOCK] = piece.astype(
                        jnp.bfloat16
                    )
            dlev_copy(j, level).start()
        for part in range(2):
            own_sum[j, part, :BLOCK] = terms[0, part, BLOCK : 2 * BLOCK] + terms[1, part, :BLOCK]
            own_sum[j, part, BLOCK:] = (
                terms[0, part, 2 * BLOCK : 3 * BLOCK] + terms[1, part, BLOCK : 2 * BLOCK]
            )

        return carry

    lax.fori_loop(0, heads, one_head, 0)

    def finish(j, carry):
        for level in range(levels):
            dlev_copy(j, level).wait_recv()

        @pl.when(has_low)
        def _():
            drim_up(j).wait_recv()

        @pl.when(has_high)
        def _():
            drim_down(j).wait_recv()

        for part in range(2):
            total = own_sum[j, part]
            for level in range(levels):
                total = total + lev_recv[level, j, part].astype(jnp.float32)
            first = total[:BLOCK] + rim_recv[0, j, part].astype(jnp.float32)
            last = total[BLOCK:] + rim_recv[1, j, part].astype(jnp.float32)
            result = (dk_ref, dv_ref)[part]
            result[j, :BLOCK] = first.astype(jnp.bfloat16)
            result[j, BLOCK:] = last.astype(jnp.bfloat16)
        for block in range(2):
            for copy in og_copies(j, block):
                copy.wait_recv()
        return carry

    lax.fori_loop(0, heads, finish, 0)

    def drain(j, carry):
        for copy in qg_copies(j) + og_copies(j, 0) + og_copies(j, 1):
            copy.wait_send()
        for level in range(levels):
            kv_copy(j, level).wait_send()
            dlev_copy(j, level).wait_send()

        @pl.when(has_high)
        def _():
            rim_up(j).wait_send()
            drim_up(j).wait_send()

        @pl.when(has_low)
        def _():
            rim_down(j).wait_send()
            drim_down(j).wait_send()

        return carry

    lax.fori_loop(0, heads, drain, 0)
    width_copy().wait_send()


def shards(query, key_in, value, grad_out, band_width, stride_bits, partner_table):
    tokens, kv_heads, groups, dim = query.shape
    heads = key_in.shape[1]
    n_seq = lax.axis_size("seq")
    levels = n_seq.bit_length() - 1
    rows = tokens * groups
    bf16 = jnp.bfloat16
    f32 = jnp.float32
    q = jnp.transpose(query, (1, 0, 2, 3)).reshape(kv_heads, rows, dim)
    g = jnp.transpose(grad_out, (1, 0, 2, 3)).reshape(kv_heads, rows, dim)
    k = jnp.transpose(key_in, (1, 0, 2))
    v = jnp.transpose(value, (1, 0, 2))
    width = jnp.pad(band_width, ((0, 0), (0, 128 - groups)))
    vmem = pl.BlockSpec(memory_space=pltpu.VMEM)
    smem = pl.BlockSpec(memory_space=pltpu.SMEM)
    slots = 3 + levels
    dma = pltpu.SemaphoreType.DMA
    out, gq, dk, dv = pl.pallas_call(
        functools.partial(kernel, n_seq, levels, heads, groups),
        out_shape=(
            jax.ShapeDtypeStruct((kv_heads, rows, dim), bf16),
            jax.ShapeDtypeStruct((kv_heads, rows, dim), bf16),
            jax.ShapeDtypeStruct((heads, tokens, dim), bf16),
            jax.ShapeDtypeStruct((heads, tokens, dim), bf16),
        ),
        in_specs=[smem, smem] + [vmem] * 5,
        out_specs=(vmem,) * 4,
        scratch_shapes=[
            pltpu.VMEM((heads, 2, tokens, dim), bf16),
            pltpu.VMEM((heads, rows, dim), bf16),
            pltpu.VMEM((heads, rows, dim), bf16),
            pltpu.VMEM((kv_heads, 128), jnp.int32),
            pltpu.VMEM((levels, heads, 2, tokens, dim), bf16),
            pltpu.VMEM((2, heads, 2, BLOCK, dim), bf16),
            pltpu.VMEM((2, slots * BLOCK, dim), bf16),
            pltpu.VMEM((2, 2, slots * BLOCK, dim), f32),
            pltpu.VMEM((heads, rows, dim), bf16),
            pltpu.VMEM((heads, rows, dim), bf16),
            pltpu.VMEM((levels, heads, 2, tokens, dim), bf16),
            pltpu.VMEM((levels, heads, 2, tokens, dim), bf16),
            pltpu.VMEM((2, heads, 2, BLOCK, dim), bf16),
            pltpu.VMEM((2, heads, 2, BLOCK, dim), bf16),
            pltpu.VMEM((heads, 2, tokens, dim), f32),
            dma((2,)),
            dma((2, 2, heads)),
            dma((2, levels, heads)),
            dma((2, 2, heads)),
            dma((2, 2, 2, heads)),
            dma((2, levels, heads)),
            dma((2, 2, heads)),
        ],
        compiler_params=pltpu.CompilerParams(
            collective_id=0, has_side_effects=True, vmem_limit_bytes=34 * 1024 * 1024
        ),
    )(partner_table, stride_bits, q, g, k, v, width)
    out = jnp.transpose(out.reshape(kv_heads, tokens, groups, dim), (1, 0, 2, 3))
    gq = jnp.transpose(gq.reshape(kv_heads, tokens, groups, dim), (1, 0, 2, 3))
    return out, gq, jnp.transpose(dk, (1, 0, 2)), jnp.transpose(dv, (1, 0, 2))


def solution(mesh):
    placed = (
        P("seq", None, "head", None),
        P("seq", "head", None),
        P("seq", "head", None),
        P("seq", None, "head", None),
        P(None, "head"),
        P(),
        P("seq", None),
    )
    return jax.shard_map(
        shards,
        mesh=mesh,
        in_specs=placed,
        out_specs=(
            P("seq", None, "head", None),
            P("seq", None, "head", None),
            P("seq", "head", None),
            P("seq", "head", None),
        ),
        check_vma=False,
    )
```
